256 devices in a mesh: band: 32 (over z, x), gvec: 8 (over y, core).
Axes of the slice: x: 4, y: 4, z: 8, core: 2. Of those that a mesh axis runs over, the one named last changes fastest.
Arguments:
- pairs: bfloat16 [32, 8, 512, 640], P(None, 'gvec', 'band'), may hold values from -0.59765625 to 0.59765625
- cond_energy: float32 [512], replicated, may hold values from 0.5 to 12
- val_energy: float32 [32, 8], replicated, may hold values from -12 to -2
- band_counts: int32 [32], replicated, may hold values from 1 to 16, as said below
- slab: int32 [1], replicated, may hold values from 0 to 31
Outputs:
- chi_zero: float32 [20480, 20480], P('gvec', 'band')
The draws below stay inside these ranges and needn't reach their ends.
Inputs may be any that keep to these rules, and one draw needn't show every extreme that they name: `band_counts`: every owner has at least one occupied slot, and in every draw some owner has all 16 slots occupied.
All inputs are finite; a program needn't handle non-finite values.
Results may differ from the reference program's by a relative error of at most 0.0028.
Values may be sent and summed in bfloat16 or wider, within the bound.
No kernel may reach another device: no remote copies, remote signals or barrier semaphores. Data moves between devices by JAX's collectives and lax.ppermute only.
A program may use at most 128 MiB of HBM per device.

```python
import jax
import jax.numpy as jnp
from jax import lax

NG = 20480
NV = 8
NSLAB = 32
CAP = 16
CBANDS = 512
N_BAND = 32


def draw_band_counts(key, part):
    first, second = jax.random.split(jax.random.fold_in(key, 11))
    base = jax.random.randint(first, (N_BAND,), 1, CAP + 1)
    fullest = jax.random.randint(second, (), 0, N_BAND)
    return jnp.where(jnp.arange(N_BAND) == fullest, CAP, base).astype(jnp.int32)


def raised(entries, rng, source, target, parts, factor):
    owner, partner = [(jnp.arange(entries.shape[position]) // (entries.shape[position] // parts)).reshape([-1 if axis == position else 1 for axis in range(entries.ndim)]) for position in (source, target)]
    chosen = jax.random.permutation(rng, parts)[partner]
    strong = (owner == chosen) | (owner == (partner + parts // 2) % parts)
    return jnp.where(strong, factor * entries, entries)


def levels(rng, shape, shards, least, largest):
    factor_of, own = 1.0, jax.random.fold_in(rng, 6)
    for position, parts in shards:
        draws = jnp.exp(jax.random.uniform(jax.random.fold_in(own, position), (parts,), jnp.float32, least / len(shards), largest / len(shards)))
        factor_of = factor_of * jnp.repeat(draws, shape[position] // parts).reshape([-1 if axis == position else 1 for axis in range(len(shape))])
    return factor_of


def noise_with(rng, extent, deviation, most, cuts, heavy, kind=jnp.bfloat16):
    drawn = deviation * jax.random.normal(rng, extent, jnp.float32)
    if cuts:
        drawn = drawn * levels(rng, extent, cuts, -0.22, 0.18)
    return jnp.clip(raised(drawn, jax.random.fold_in(rng, 3), *heavy), -most, most).astype(kind)


def setup_inputs(seed: int = 0) -> dict:
    keys = jax.random.split(jax.random.key(seed), 6)
    return {
        "pairs": noise_with(keys[0], (N_BAND, NV, CBANDS, NG // N_BAND), 0.1, 0.59765625, ((1, 8), (2, 32)), (2, 0, 32, 2.75)),
        "cond_energy": jnp.clip(jax.random.uniform(keys[1], (CBANDS,), jnp.float32, 0.5, 12.0), 0.5, 12.0),
        "val_energy": jnp.clip(jax.random.uniform(keys[2], (NSLAB, NV), jnp.float32, -12.0, -2.0), -12.0, -2.0),
        "band_counts": draw_band_counts(jax.random.fold_in(keys[5], 71), 0),
        "slab": jax.random.randint(keys[4], (1,), 0, NSLAB).astype(jnp.int32),
    }


def reference(pairs, cond_energy, val_energy, band_counts, slab):
    energies = lax.dynamic_index_in_dim(val_energy, slab[0].astype(jnp.int32), 0, keepdims=False)
    slots = jnp.arange(CAP, dtype=jnp.int32)
    live = (slots[None, :] < band_counts[:, None]).reshape(-1)
    weight = jnp.where(live[None, :], 2.0 / (energies[:, None] - cond_energy[None, :]), jnp.float32(0.0)).astype(jnp.float32)
    scaled = (weight[None, :, :, None] * pairs.astype(jnp.float32)).astype(jnp.bfloat16)
    blocks = pairs.shape[0]
    width = pairs.shape[3]
    flat_rows = jnp.transpose(pairs, (1, 2, 0, 3)).reshape(-1, blocks * width)
    flat_cols = jnp.transpose(scaled, (1, 2, 0, 3)).reshape(-1, blocks * width)
    return lax.dot_general(flat_rows, flat_cols, (((0,), (0,)), ((), ())), preferred_element_type=jnp.float32)
```

```python
import functools

import jax
import jax.numpy as jnp
from jax import lax
from jax.experimental import pallas as pl
from jax.experimental.pallas import tpu as pltpu
from jax.sharding import PartitionSpec as P

BUCKETS = (192, 224, 240, 256, 272, 288, 304, 320, 352, 384, 448, 512)
Z, X = 8, 4
WIDE = 384
VMEM_BYTES = 48 * 1024 * 1024
BOTH = ("band", "gvec")
ALONG_Z = [[z * X + x for z in range(Z)] for x in range(X)]


def band_of(z, x):
    return (z % Z) * X + x % X


def shift(value, dz, dx):
    pairs = [(band_of(z + dz, x + dx), band_of(z, x)) for z in range(Z) for x in range(X)]
    return lax.ppermute(value, "band", pairs)


def to_rows(value):
    moves = [
        (band_of(z, x) * Z + v, band_of(z, x) * Z + (z - v) % Z)
        for z in range(Z) for x in range(X) for v in range(Z)
    ]
    return lax.ppermute(value, BOTH, moves)


def to_cols(value):
    moves = [
        (band_of(z, x) * Z + v, band_of(z - v, x) * Z + v)
        for z in range(Z) for x in range(X) for v in range(Z)
    ]
    return lax.ppermute(value, BOTH, moves)


def cut_of(depth):
    return depth // 32 * 16


def low_of(value):
    return value[:cut_of(value.shape[0])]


def high_of(value):
    return value[cut_of(value.shape[0]):]


def together(*values):
    return lax.optimization_barrier(values)


def from_y(value, dy):
    return lax.ppermute(value, "gvec", [((i + 2 * dy) % Z, i) for i in range(Z)])


def contract(left, right):
    return lax.dot_general(left, right, (((0,), (0,)), ((), ())), preferred_element_type=jnp.float32)


def sum_kernel(offsets, width, parts, adds, aliased, where, cols, *refs):
    refs = list(refs)
    lefts = [refs.pop(0) for _ in offsets]
    partial = refs.pop(0) if adds else None
    if aliased:
        refs.pop(0)
    out, acc, sems = refs
    total = None
    for offset, left in zip(offsets, lefts):
        term = contract(left[...], cols[offset:offset + left.shape[0], :])
        total = term if total is None else total + term
    if adds:
        total = total + partial[...]
    acc[...] = total
    copies = []
    for i in range(parts):
        start = pl.multiple_of(where[i], 128)
        copies.append(
            pltpu.make_async_copy(acc.at[pl.ds(i * width, width)], out.at[pl.ds(start, width)], sems.at[i])
        )
        copies[-1].start()
    for copy in copies:
        copy.wait()


def add_rows(out, where, cols, lefts, offsets, parts, partial=None, size=None):
    height, n = lefts[0].shape[1], cols.shape[1]
    width = height // parts
    vmem = pl.BlockSpec(memory_space=pltpu.VMEM)
    operands = [where, cols, *lefts] + ([] if partial is None else [partial])
    specs = [pl.BlockSpec(memory_space=pltpu.SMEM)] + [vmem] * (len(operands) - 1)
    alias = {}
    if out is not None:
        alias = {len(operands): 0}
        operands.append(out)
        specs.append(pl.BlockSpec(memory_space=pl.ANY))
        size = out.shape
    depth = sum(left.shape[0] for left in lefts)
    return pl.pallas_call(
        functools.partial(sum_kernel, offsets, width, parts, partial is not None, out is not None),
        out_shape=jax.ShapeDtypeStruct(size, jnp.float32),
        in_specs=specs,
        out_specs=pl.BlockSpec(memory_space=pl.ANY),
        scratch_shapes=[pltpu.VMEM((height, n), jnp.float32), pltpu.SemaphoreType.DMA((parts,))],
        input_output_aliases=alias,
        compiler_params=pltpu.CompilerParams(vmem_limit_bytes=VMEM_BYTES),
        cost_estimate=pl.CostEstimate(
            flops=2 * depth * height * n, bytes_accessed=2 * depth * (height + n) + 4 * height * n, transcendentals=0
        ),
    )(*operands)


def rows_kernel(width, where, cols, rows, _, out, acc, sems):
    j, slot = pl.program_id(0), pl.program_id(0) % 2

    def store(step):
        start = pl.multiple_of(where[step], 128)
        return pltpu.make_async_copy(acc.at[step % 2], out.at[pl.ds(start, width)], sems.at[step % 2])

    @pl.when(j >= 2)
    def _():
        store(j - 2).wait()

    acc[slot] = contract(rows[...].reshape(cols.shape[0], width), cols[...])
    store(j).start()

    @pl.when(j == X - 1)
    def _():
        store(j - 1).wait()
        store(j).wait()


def add_gathered(out, where, cols, rows):
    depth, n = rows.shape[1], cols.shape[1]
    width = rows.shape[2] // X
    return pl.pallas_call(
        functools.partial(rows_kernel, width),
        grid=(X,),
        out_shape=jax.ShapeDtypeStruct(out.shape, jnp.float32),
        in_specs=[
            pl.BlockSpec(memory_space=pltpu.SMEM),
            pl.BlockSpec(cols.shape, lambda j: (0, 0)),
            pl.BlockSpec((Z, depth, width), lambda j: (0, 0, j)),
            pl.BlockSpec(memory_space=pl.ANY),
        ],
        out_specs=pl.BlockSpec(memory_space=pl.ANY),
        scratch_shapes=[pltpu.VMEM((2, width, n), jnp.float32), pltpu.SemaphoreType.DMA((2,))],
        input_output_aliases={3: 0},
        compiler_params=pltpu.CompilerParams(vmem_limit_bytes=VMEM_BYTES),
        cost_estimate=pl.CostEstimate(
            flops=2 * X * Z * depth * width * n, bytes_accessed=2 * X * Z * depth * (width + n), transcendentals=0
        ),
    )(where, cols, rows, out)


def order_kernel(depth, order, half, other, out, sems):
    def copies(source, wanted):
        for i in range(Z):
            place = order[i]

            @pl.when((place >= X) == wanted)
            def _():
                start = pl.multiple_of(place % X * depth, 16)
                pltpu.make_async_copy(
                    source.at[pl.ds(start, depth)], out.at[pl.ds(i * depth, depth)], sems.at[i]
                ).start()

    copies(half, False)
    copies(other, True)
    for i in range(Z):
        pltpu.make_async_copy(half.at[pl.ds(0, depth)], out.at[pl.ds(i * depth, depth)], sems.at[i]).wait()


def reorder(order, half, other):
    depth, n = half.shape[0] // X, half.shape[1]
    return pl.pallas_call(
        functools.partial(order_kernel, depth),
        out_shape=jax.ShapeDtypeStruct((Z * depth, n), half.dtype),
        in_specs=[pl.BlockSpec(memory_space=pltpu.SMEM)] + [pl.BlockSpec(memory_space=pl.ANY)] * 2,
        out_specs=pl.BlockSpec(memory_space=pltpu.VMEM),
        scratch_shapes=[pltpu.SemaphoreType.DMA((Z,))],
        compiler_params=pltpu.CompilerParams(vmem_limit_bytes=VMEM_BYTES),
        cost_estimate=pl.CostEstimate(flops=0, bytes_accessed=4 * Z * depth * n, transcendentals=0),
    )(order, half, other)


def with_offsets(at, *lefts):
    offsets = []
    for left in lefts:
        offsets.append(at)
        at += left.shape[0]
    return lefts, offsets


def with_slots(depth, block, weight, place):
    gvec, band = lax.axis_index("gvec"), lax.axis_index("band")
    z, x = band // X, band % X
    n = block.shape[1]
    rows_of = jnp.arange(depth, dtype=jnp.int32)
    select = (rows_of[:, None] == place[None, :]).astype(jnp.bfloat16)
    packed = jnp.dot(select, block, preferred_element_type=jnp.float32).astype(jnp.bfloat16)
    scaled = (weight[:, None] * block.astype(jnp.float32)).astype(jnp.bfloat16)
    packed_cols = jnp.dot(select, scaled, preferred_element_type=jnp.float32).astype(jnp.bfloat16)

    mine = to_cols(packed_cols)
    a0 = to_rows(packed[:, :WIDE])
    b0 = to_rows(packed[:, WIDE:])
    a0, b0, mine = together(a0, b0, mine)

    b1, b3 = shift(b0, 0, 1), shift(b0, 0, -1)
    up1, down1 = shift(a0, 1, 0), shift(a0, -1, 0)
    y1 = from_y(mine, 1)
    b1, b3, up1, down1, y1 = together(b1, b3, up1, down1, y1)

    b2 = jnp.concatenate([shift(low_of(b1), 0, 1), shift(high_of(b3), 0, -1)], axis=0)
    b = jnp.concatenate([b0, b1, b2, b3], axis=1)
    up2, down2 = shift(up1, 1, 0), shift(down1, -1, 0)
    first = jnp.concatenate([a0, up1, down1], axis=0)
    y3 = from_y(mine, -1)
    b, up2, down2, first, y3 = together(b, up2, down2, first, y3)
    b_all = lax.all_gather(b, "band", axis=0, axis_index_groups=ALONG_Z)

    near1, far1 = shift(first, 0, 1), shift(first, 0, -1)
    up3, down3 = shift(up2, 1, 0), shift(down2, -1, 0)
    y2 = from_y(mine, 2)
    half = jnp.concatenate([mine, y1, y2, y3], axis=0)
    near1, far1, up3, down3, half = together(near1, far1, up3, down3, half)

    cross1 = [shift(low_of(near1), 0, 1), shift(high_of(far1), 0, -1)]
    last = [shift(low_of(up3), 1, 0), shift(high_of(down3), -1, 0)]
    second = jnp.concatenate([up2, down2, up3, down3, *last], axis=0)
    other = lax.ppermute(half, "gvec", [(i ^ 1, i) for i in range(Z)])
    low1, high1, second, half, other = together(*cross1, second, half, other)

    y, core = gvec // 2, gvec % 2

    def ordered(positions):
        wanted = (positions - gvec + 2 * Z) % Z
        return reorder((wanted // 2 - y + X) % X + X * (wanted % 2 != core).astype(jnp.int32), half, other)

    def starts(shifts, base):
        return jnp.stack([(x + s) % X * n + base for s in shifts]).astype(jnp.int32)

    near2, far2 = shift(second, 0, 1), shift(second, 0, -1)
    near_cols = ordered(z + jnp.array([0, 1, 7, 2, 6, 3, 5, 4], jnp.int32))
    in_cols = ordered(jnp.arange(Z, dtype=jnp.int32))
    out = add_rows(None, starts([0], 0), near_cols, *with_offsets(0, first, second), 1, size=(X * n, n))
    near2, far2, out, near_cols, in_cols = together(near2, far2, out, near_cols, in_cols)

    low2, high2 = shift(low_of(near2), 0, 1), shift(high_of(far2), 0, -1)
    out = add_rows(out, starts([1], 0), near_cols, *with_offsets(0, near1, near2), 1)
    out = add_rows(out, starts([3], 0), near_cols, *with_offsets(0, far1, far2), 1)
    out = add_gathered(out, starts([0, 1, 2, 3], WIDE), in_cols, b_all)
    low2, high2, out = together(low2, high2, out)
    return add_rows(out, starts([2], 0), near_cols, *with_offsets(0, low1, high1, low2, high2), 1)


def on_device(pairs, cond_energy, val_energy, band_counts, slab):
    gvec = lax.axis_index("gvec")
    blocks, _, slots, n = pairs.shape
    energies = lax.dynamic_index_in_dim(val_energy, slab[0], 0, keepdims=False)
    energy = lax.dynamic_index_in_dim(energies, gvec, 0, keepdims=False)
    live = (jnp.arange(slots, dtype=jnp.int32)[None, :] < band_counts[:, None]).reshape(-1)
    weight = jnp.where(live, 2.0 / (energy - cond_energy), jnp.float32(0.0))
    owners = jnp.arange(band_counts.shape[0])
    before = jnp.sum(jnp.where(owners[None, :] < owners[:, None], band_counts[None, :], 0), axis=1)
    place = jnp.where(
        live, (before[:, None] + jnp.arange(slots, dtype=jnp.int32)[None, :]).reshape(-1), -1
    )
    total = jnp.sum(band_counts)

    rolled = jnp.roll(pairs.reshape(Z, X, slots, n), gvec, axis=0).reshape(blocks, slots, n)
    block = lax.all_to_all(rolled, "band", split_axis=0, concat_axis=0, tiled=True)
    block = block.reshape(blocks * slots, n)
    block, weight, place, total = together(block, weight, place, total)
    which = sum((total > b).astype(jnp.int32) for b in BUCKETS[:-1])
    return lax.switch(which, [functools.partial(with_slots, b) for b in BUCKETS], block, weight, place)


def solution(mesh):
    in_specs = (P(None, "gvec", "band", None), P(), P(), P(), P())
    out_specs = P("gvec", "band")
    return jax.shard_map(
        on_device, mesh=mesh, in_specs=in_specs, out_specs=out_specs, check_vma=False
    )
```

```python
import functools

import jax
import jax.numpy as jnp
from jax import lax
from jax.experimental import pallas as pl
from jax.experimental.pallas import tpu as pltpu
from jax.sharding import PartitionSpec as P

BUCKETS = (320, 512)
Z, X = 8, 4
WIDE = 384
VMEM_BYTES = 48 * 1024 * 1024
BOTH = ("band", "gvec")
ALONG_Z = [[z * X + x for z in range(Z)] for x in range(X)]


def band_of(z, x):
    return (z % Z) * X + x % X


def shift(value, dz, dx):
    pairs = [(band_of(z + dz, x + dx), band_of(z, x)) for z in range(Z) for x in range(X)]
    return lax.ppermute(value, "band", pairs)


def to_rows(value):
    moves = [
        (band_of(z, x) * Z + v, band_of(z, x) * Z + (z - v) % Z)
        for z in range(Z) for x in range(X) for v in range(Z)
    ]
    return lax.ppermute(value, BOTH, moves)


def to_cols(value):
    moves = [
        (band_of(z, x) * Z + v, band_of(z - v, x) * Z + v)
        for z in range(Z) for x in range(X) for v in range(Z)
    ]
    return lax.ppermute(value, BOTH, moves)


def cut_of(depth):
    return depth // 32 * 16


def low_of(value):
    return value[:cut_of(value.shape[0])]


def high_of(value):
    return value[cut_of(value.shape[0]):]


def together(*values):
    return lax.optimization_barrier(values)


def from_y(value, dy):
    return lax.ppermute(value, "gvec", [((i + 2 * dy) % Z, i) for i in range(Z)])


def contract(left, right):
    return lax.dot_general(left, right, (((0,), (0,)), ((), ())), preferred_element_type=jnp.float32)


def sum_kernel(offsets, width, parts, adds, aliased, where, cols, *refs):
    refs = list(refs)
    lefts = [refs.pop(0) for _ in offsets]
    partial = refs.pop(0) if adds else None
    if aliased:
        refs.pop(0)
    out, acc, sems = refs
    total = None
    for offset, left in zip(offsets, lefts):
        term = contract(left[...], cols[offset:offset + left.shape[0], :])
        total = term if total is None else total + term
    if adds:
        total = total + partial[...]
    acc[...] = total
    copies = []
    for i in range(parts):
        start = pl.multiple_of(where[i], 128)
        copies.append(
            pltpu.make_async_copy(acc.at[pl.ds(i * width, width)], out.at[pl.ds(start, width)], sems.at[i])
        )
        copies[-1].start()
    for copy in copies:
        copy.wait()


def add_rows(out, where, cols, lefts, offsets, parts, partial=None, size=None):
    height, n = lefts[0].shape[1], cols.shape[1]
    width = height // parts
    vmem = pl.BlockSpec(memory_space=pltpu.VMEM)
    operands = [where, cols, *lefts] + ([] if partial is None else [partial])
    specs = [pl.BlockSpec(memory_space=pltpu.SMEM)] + [vmem] * (len(operands) - 1)
    alias = {}
    if out is not None:
        alias = {len(operands): 0}
        operands.append(out)
        specs.append(pl.BlockSpec(memory_space=pl.ANY))
        size = out.shape
    depth = sum(left.shape[0] for left in lefts)
    return pl.pallas_call(
        functools.partial(sum_kernel, offsets, width, parts, partial is not None, out is not None),
        out_shape=jax.ShapeDtypeStruct(size, jnp.float32),
        in_specs=specs,
        out_specs=pl.BlockSpec(memory_space=pl.ANY),
        scratch_shapes=[pltpu.VMEM((height, n), jnp.float32), pltpu.SemaphoreType.DMA((parts,))],
        input_output_aliases=alias,
        compiler_params=pltpu.CompilerParams(vmem_limit_bytes=VMEM_BYTES),
        cost_estimate=pl.CostEstimate(
            flops=2 * depth * height * n, bytes_accessed=2 * depth * (height + n) + 4 * height * n, transcendentals=0
        ),
    )(*operands)


def rows_kernel(width, where, cols, rows, _, out, acc, sems):
    j, slot = pl.program_id(0), pl.program_id(0) % 2

    def store(step):
        start = pl.multiple_of(where[step], 128)
        return pltpu.make_async_copy(acc.at[step % 2], out.at[pl.ds(start, width)], sems.at[step % 2])

    @pl.when(j >= 2)
    def _():
        store(j - 2).wait()

    acc[slot] = contract(rows[...].reshape(cols.shape[0], width), cols[...])
    store(j).start()

    @pl.when(j == X - 1)
    def _():
        store(j - 1).wait()
        store(j).wait()


def add_gathered(out, where, cols, rows):
    depth, n = rows.shape[1], cols.shape[1]
    width = rows.shape[2] // X
    return pl.pallas_call(
        functools.partial(rows_kernel, width),
        grid=(X,),
        out_shape=jax.ShapeDtypeStruct(out.shape, jnp.float32),
        in_specs=[
            pl.BlockSpec(memory_space=pltpu.SMEM),
            pl.BlockSpec(cols.shape, lambda j: (0, 0)),
            pl.BlockSpec((Z, depth, width), lambda j: (0, 0, j)),
            pl.BlockSpec(memory_space=pl.ANY),
        ],
        out_specs=pl.BlockSpec(memory_space=pl.ANY),
        scratch_shapes=[pltpu.VMEM((2, width, n), jnp.float32), pltpu.SemaphoreType.DMA((2,))],
        input_output_aliases={3: 0},
        compiler_params=pltpu.CompilerParams(vmem_limit_bytes=VMEM_BYTES),
        cost_estimate=pl.CostEstimate(
            flops=2 * X * Z * depth * width * n, bytes_accessed=2 * X * Z * depth * (width + n), transcendentals=0
        ),
    )(where, cols, rows, out)


def order_kernel(depth, order, half, other, out, sems):
    def copies(source, wanted):
        for i in range(Z):
            place = order[i]

            @pl.when((place >= X) == wanted)
            def _():
                start = pl.multiple_of(place % X * depth, 16)
                pltpu.make_async_copy(
                    source.at[pl.ds(start, depth)], out.at[pl.ds(i * depth, depth)], sems.at[i]
                ).start()

    copies(half, False)
    copies(other, True)
    for i in range(Z):
        pltpu.make_async_copy(half.at[pl.ds(0, depth)], out.at[pl.ds(i * depth, depth)], sems.at[i]).wait()


def reorder(order, half, other):
    depth, n = half.shape[0] // X, half.shape[1]
    return pl.pallas_call(
        functools.partial(order_kernel, depth),
        out_shape=jax.ShapeDtypeStruct((Z * depth, n), half.dtype),
        in_specs=[pl.BlockSpec(memory_space=pltpu.SMEM)] + [pl.BlockSpec(memory_space=pl.ANY)] * 2,
        out_specs=pl.BlockSpec(memory_space=pltpu.VMEM),
        scratch_shapes=[pltpu.SemaphoreType.DMA((Z,))],
        compiler_params=pltpu.CompilerParams(vmem_limit_bytes=VMEM_BYTES),
        cost_estimate=pl.CostEstimate(flops=0, bytes_accessed=4 * Z * depth * n, transcendentals=0),
    )(order, half, other)


def with_offsets(at, *lefts):
    offsets = []
    for left in lefts:
        offsets.append(at)
        at += left.shape[0]
    return lefts, offsets


def with_slots(depth, block, weight, place):
    gvec, band = lax.axis_index("gvec"), lax.axis_index("band")
    z, x = band // X, band % X
    n = block.shape[1]
    rows_of = jnp.arange(depth, dtype=jnp.int32)
    select = (rows_of[:, None] == place[None, :]).astype(jnp.bfloat16)
    packed = jnp.dot(select, block, preferred_element_type=jnp.float32).astype(jnp.bfloat16)
    scaled = (weight[:, None] * block.astype(jnp.float32)).astype(jnp.bfloat16)
    packed_cols = jnp.dot(select, scaled, preferred_element_type=jnp.float32).astype(jnp.bfloat16)

    mine = to_cols(packed_cols)
    a0 = to_rows(packed[:, :WIDE])
    b0 = to_rows(packed[:, WIDE:])
    a0, b0, mine = together(a0, b0, mine)

    b1, b3 = shift(b0, 0, 1), shift(b0, 0, -1)
    up1, down1 = shift(a0, 1, 0), shift(a0, -1, 0)
    y1 = from_y(mine, 1)
    b1, b3, up1, down1, y1 = together(b1, b3, up1, down1, y1)

    b2 = jnp.concatenate([shift(low_of(b1), 0, 1), shift(high_of(b3), 0, -1)], axis=0)
    b = jnp.concatenate([b0, b1, b2, b3], axis=1)
    up2, down2 = shift(up1, 1, 0), shift(down1, -1, 0)
    first = jnp.concatenate([a0, up1, down1], axis=0)
    y3 = from_y(mine, -1)
    b, up2, down2, first, y3 = together(b, up2, down2, first, y3)
    b_all = lax.all_gather(b, "band", axis=0, axis_index_groups=ALONG_Z)

    near1, far1 = shift(first, 0, 1), shift(first, 0, -1)
    up3, down3 = shift(up2, 1, 0), shift(down2, -1, 0)
    y2 = from_y(mine, 2)
    half = jnp.concatenate([mine, y1, y2, y3], axis=0)
    near1, far1, up3, down3, half = together(near1, far1, up3, down3, half)

    cross1 = [shift(low_of(near1), 0, 1), shift(high_of(far1), 0, -1)]
    last = [shift(low_of(up3), 1, 0), shift(high_of(down3), -1, 0)]
    second = jnp.concatenate([up2, down2, up3, down3, *last], axis=0)
    other = lax.ppermute(half, "gvec", [(i ^ 1, i) for i in range(Z)])
    low1, high1, second, half, other = together(*cross1, second, half, other)

    y, core = gvec // 2, gvec % 2

    def ordered(positions):
        wanted = (positions - gvec + 2 * Z) % Z
        return reorder((wanted // 2 - y + X) % X + X * (wanted % 2 != core).astype(jnp.int32), half, other)

    def starts(shifts, base):
        return jnp.stack([(x + s) % X * n + base for s in shifts]).astype(jnp.int32)

    near2, far2 = shift(second, 0, 1), shift(second, 0, -1)
    near_cols = ordered(z + jnp.array([0, 1, 7, 2, 6, 3, 5, 4], jnp.int32))
    in_cols = ordered(jnp.arange(Z, dtype=jnp.int32))
    out = add_rows(None, starts([0], 0), near_cols, *with_offsets(0, first, second), 1, size=(X * n, n))
    near2, far2, out, near_cols, in_cols = together(near2, far2, out, near_cols, in_cols)

    low2, high2 = shift(low_of(near2), 0, 1), shift(high_of(far2), 0, -1)
    out = add_rows(out, starts([1], 0), near_cols, *with_offsets(0, near1, near2), 1)
    out = add_rows(out, starts([3], 0), near_cols, *with_offsets(0, far1, far2), 1)
    out = add_gathered(out, starts([0, 1, 2, 3], WIDE), in_cols, b_all)
    low2, high2, out = together(low2, high2, out)
    return add_rows(out, starts([2], 0), near_cols, *with_offsets(0, low1, high1, low2, high2), 1)


def on_device(pairs, cond_energy, val_energy, band_counts, slab):
    gvec = lax.axis_index("gvec")
    blocks, _, slots, n = pairs.shape
    energies = lax.dynamic_index_in_dim(val_energy, slab[0], 0, keepdims=False)
    energy = lax.dynamic_index_in_dim(energies, gvec, 0, keepdims=False)
    live = (jnp.arange(slots, dtype=jnp.int32)[None, :] < band_counts[:, None]).reshape(-1)
    weight = jnp.where(live, 2.0 / (energy - cond_energy), jnp.float32(0.0))
    owners = jnp.arange(band_counts.shape[0])
    before = jnp.sum(jnp.where(owners[None, :] < owners[:, None], band_counts[None, :], 0), axis=1)
    place = jnp.where(
        live, (before[:, None] + jnp.arange(slots, dtype=jnp.int32)[None, :]).reshape(-1), -1
    )
    total = jnp.sum(band_counts)

    rolled = jnp.roll(pairs.reshape(Z, X, slots, n), gvec, axis=0).reshape(blocks, slots, n)
    block = lax.all_to_all(rolled, "band", split_axis=0, concat_axis=0, tiled=True)
    block = block.reshape(blocks * slots, n)
    block, weight, place, total = together(block, weight, place, total)
    which = sum((total > b).astype(jnp.int32) for b in BUCKETS[:-1])
    return lax.switch(which, [functools.partial(with_slots, b) for b in BUCKETS], block, weight, place)


def solution(mesh):
    in_specs = (P(None, "gvec", "band", None), P(), P(), P(), P())
    out_specs = P("gvec", "band")
    return jax.shard_map(
        on_device, mesh=mesh, in_specs=in_specs, out_specs=out_specs, check_vma=False
    )
```

```python
import functools

import jax
import jax.numpy as jnp
from jax import lax
from jax.experimental import pallas as pl
from jax.experimental.pallas import tpu as pltpu
from jax.sharding import PartitionSpec as P

BUCKETS = (288, 336, 512)
Z, X = 8, 4
WIDE = 384
VMEM_BYTES = 48 * 1024 * 1024
BOTH = ("band", "gvec")
ALONG_Z = [[z * X + x for z in range(Z)] for x in range(X)]


def band_of(z, x):
    return (z % Z) * X + x % X


def shift(value, dz, dx):
    pairs = [(band_of(z + dz, x + dx), band_of(z, x)) for z in range(Z) for x in range(X)]
    return lax.ppermute(value, "band", pairs)


def to_rows(value):
    moves = [
        (band_of(z, x) * Z + v, band_of(v, x) * Z + z)
        for z in range(Z) for x in range(X) for v in range(Z)
    ]
    return lax.ppermute(value, BOTH, moves)


def cut_of(depth):
    return depth // 32 * 16


def low_of(value):
    return value[:cut_of(value.shape[0])]


def high_of(value):
    return value[cut_of(value.shape[0]):]


def together(*values):
    return lax.optimization_barrier(values)


def from_y(value, dy):
    return lax.ppermute(value, "gvec", [((i + 2 * dy) % Z, i) for i in range(Z)])


def contract(left, right):
    return lax.dot_general(left, right, (((0,), (0,)), ((), ())), preferred_element_type=jnp.float32)


def sum_kernel(offsets, width, parts, adds, aliased, where, cols, *refs):
    refs = list(refs)
    lefts = [refs.pop(0) for _ in offsets]
    partial = refs.pop(0) if adds else None
    if aliased:
        refs.pop(0)
    out, acc, sems = refs
    total = None
    for offset, left in zip(offsets, lefts):
        term = contract(left[...], cols[offset:offset + left.shape[0], :])
        total = term if total is None else total + term
    if adds:
        total = total + partial[...]
    acc[...] = total
    copies = []
    for i in range(parts):
        start = pl.multiple_of(where[i], 128)
        copies.append(
            pltpu.make_async_copy(acc.at[pl.ds(i * width, width)], out.at[pl.ds(start, width)], sems.at[i])
        )
        copies[-1].start()
    for copy in copies:
        copy.wait()


def add_rows(out, where, cols, lefts, offsets, parts, partial=None, size=None):
    height, n = lefts[0].shape[1], cols.shape[1]
    width = height // parts
    vmem = pl.BlockSpec(memory_space=pltpu.VMEM)
    operands = [where, cols, *lefts] + ([] if partial is None else [partial])
    specs = [pl.BlockSpec(memory_space=pltpu.SMEM)] + [vmem] * (len(operands) - 1)
    alias = {}
    if out is not None:
        alias = {len(operands): 0}
        operands.append(out)
        specs.append(pl.BlockSpec(memory_space=pl.ANY))
        size = out.shape
    depth = sum(left.shape[0] for left in lefts)
    return pl.pallas_call(
        functools.partial(sum_kernel, offsets, width, parts, partial is not None, out is not None),
        out_shape=jax.ShapeDtypeStruct(size, jnp.float32),
        in_specs=specs,
        out_specs=pl.BlockSpec(memory_space=pl.ANY),
        scratch_shapes=[pltpu.VMEM((height, n), jnp.float32), pltpu.SemaphoreType.DMA((parts,))],
        input_output_aliases=alias,
        compiler_params=pltpu.CompilerParams(vmem_limit_bytes=VMEM_BYTES),
        cost_estimate=pl.CostEstimate(
            flops=2 * depth * height * n, bytes_accessed=2 * depth * (height + n) + 4 * height * n, transcendentals=0
        ),
    )(*operands)


def rows_kernel(width, where, cols, rows, _, out, acc, sems):
    j, slot = pl.program_id(0), pl.program_id(0) % 2

    def store(step):
        start = pl.multiple_of(where[step], 128)
        return pltpu.make_async_copy(acc.at[step % 2], out.at[pl.ds(start, width)], sems.at[step % 2])

    @pl.when(j >= 2)
    def _():
        store(j - 2).wait()

    acc[slot] = contract(rows[...].reshape(cols.shape[0], width), cols[...])
    store(j).start()

    @pl.when(j == X - 1)
    def _():
        store(j - 1).wait()
        store(j).wait()


def add_gathered(out, where, cols, rows):
    depth, n = rows.shape[1], cols.shape[1]
    width = rows.shape[2] // X
    return pl.pallas_call(
        functools.partial(rows_kernel, width),
        grid=(X,),
        out_shape=jax.ShapeDtypeStruct(out.shape, jnp.float32),
        in_specs=[
            pl.BlockSpec(memory_space=pltpu.SMEM),
            pl.BlockSpec(cols.shape, lambda j: (0, 0)),
            pl.BlockSpec((Z, depth, width), lambda j: (0, 0, j)),
            pl.BlockSpec(memory_space=pl.ANY),
        ],
        out_specs=pl.BlockSpec(memory_space=pl.ANY),
        scratch_shapes=[pltpu.VMEM((2, width, n), jnp.float32), pltpu.SemaphoreType.DMA((2,))],
        input_output_aliases={3: 0},
        compiler_params=pltpu.CompilerParams(vmem_limit_bytes=VMEM_BYTES),
        cost_estimate=pl.CostEstimate(
            flops=2 * X * Z * depth * width * n, bytes_accessed=2 * X * Z * depth * (width + n), transcendentals=0
        ),
    )(where, cols, rows, out)


def order_kernel(depth, order, half, other, out, sems):
    def copies(source, wanted):
        for i in range(Z):
            place = order[i]

            @pl.when((place >= X) == wanted)
            def _():
                start = pl.multiple_of(place % X * depth, 16)
                pltpu.make_async_copy(
                    source.at[pl.ds(start, depth)], out.at[pl.ds(i * depth, depth)], sems.at[i]
                ).start()

    copies(half, False)
    copies(other, True)
    for i in range(Z):
        pltpu.make_async_copy(half.at[pl.ds(0, depth)], out.at[pl.ds(i * depth, depth)], sems.at[i]).wait()


def reorder(order, half, other):
    depth, n = half.shape[0] // X, half.shape[1]
    return pl.pallas_call(
        functools.partial(order_kernel, depth),
        out_shape=jax.ShapeDtypeStruct((Z * depth, n), half.dtype),
        in_specs=[pl.BlockSpec(memory_space=pltpu.SMEM)] + [pl.BlockSpec(memory_space=pl.ANY)] * 2,
        out_specs=pl.BlockSpec(memory_space=pltpu.VMEM),
        scratch_shapes=[pltpu.SemaphoreType.DMA((Z,))],
        compiler_params=pltpu.CompilerParams(vmem_limit_bytes=VMEM_BYTES),
        cost_estimate=pl.CostEstimate(flops=0, bytes_accessed=4 * Z * depth * n, transcendentals=0),
    )(order, half, other)


def with_offsets(at, *lefts):
    offsets = []
    for left in lefts:
        offsets.append(at)
        at += left.shape[0]
    return lefts, offsets


def with_slots(depth, block, weight, place):
    gvec, band = lax.axis_index("gvec"), lax.axis_index("band")
    x = band % X
    n = block.shape[1]
    rows_of = jnp.arange(depth, dtype=jnp.int32)
    select = (rows_of[:, None] == place[None, :]).astype(jnp.bfloat16)
    packed = jnp.dot(select, block, preferred_element_type=jnp.float32).astype(jnp.bfloat16)
    scaled = (weight[:, None] * block.astype(jnp.float32)).astype(jnp.bfloat16)
    packed_cols = jnp.dot(select, scaled, preferred_element_type=jnp.float32).astype(jnp.bfloat16)

    a0 = to_rows(packed[:, :WIDE])
    a_all = lax.all_gather(a0, "band", axis=0, axis_index_groups=ALONG_Z, tiled=True)
    b0 = to_rows(packed[:, WIDE:])
    mine = packed_cols

    b1, b3 = shift(b0, 0, 1), shift(b0, 0, -1)
    y2 = from_y(mine, 2)
    b1, b3, y2 = together(b1, b3, y2)
    b2 = jnp.concatenate([shift(low_of(b1), 0, 1), shift(high_of(b3), 0, -1)], axis=0)
    b = jnp.concatenate([b0, b1, b2, b3], axis=1)
    y1, y3 = from_y(mine, 1), from_y(mine, -1)
    b, y1, y3 = together(b, y1, y3)
    b_all = lax.all_gather(b, "band", axis=0, axis_index_groups=ALONG_Z)
    half = jnp.concatenate([mine, y1, y2, y3], axis=0)
    other = lax.ppermute(half, "gvec", [(i ^ 1, i) for i in range(Z)])

    y, core = gvec // 2, gvec % 2
    wanted = jnp.arange(Z, dtype=jnp.int32)
    cols = reorder((wanted // 2 - y + X) % X + X * (wanted % 2 != core).astype(jnp.int32), half, other)

    def starts(shifts, base):
        return jnp.stack([(x + s) % X * n + base for s in shifts]).astype(jnp.int32)

    a_all, cols = together(a_all, cols)
    near, far = shift(a_all, 0, 1), shift(a_all, 0, -1)
    out = add_rows(None, starts([0], 0), cols, *with_offsets(0, a_all), 1, size=(X * n, n))
    near, far, out = together(near, far, out)

    low, high = shift(low_of(near), 0, 1), shift(high_of(far), 0, -1)
    out = add_rows(out, starts([1], 0), cols, *with_offsets(0, near), 1)
    out = add_rows(out, starts([3], 0), cols, *with_offsets(0, far), 1)
    out = add_gathered(out, starts([0, 1, 2, 3], WIDE), cols, b_all)
    return add_rows(out, starts([2], 0), cols, *with_offsets(0, low, high), 1)


def on_device(pairs, cond_energy, val_energy, band_counts, slab):
    gvec = lax.axis_index("gvec")
    blocks, _, slots, n = pairs.shape
    energies = lax.dynamic_index_in_dim(val_energy, slab[0], 0, keepdims=False)
    energy = lax.dynamic_index_in_dim(energies, gvec, 0, keepdims=False)
    live = (jnp.arange(slots, dtype=jnp.int32)[None, :] < band_counts[:, None]).reshape(-1)
    weight = jnp.where(live, 2.0 / (energy - cond_energy), jnp.float32(0.0))
    owners = jnp.arange(band_counts.shape[0])
    before = jnp.sum(jnp.where(owners[None, :] < owners[:, None], band_counts[None, :], 0), axis=1)
    place = jnp.where(
        live, (before[:, None] + jnp.arange(slots, dtype=jnp.int32)[None, :]).reshape(-1), -1
    )
    total = jnp.sum(band_counts)

    block = lax.all_to_all(pairs.reshape(blocks, slots, n), "band", split_axis=0, concat_axis=0, tiled=True)
    block = block.reshape(blocks * slots, n)
    block, weight, place, total = together(block, weight, place, total)
    which = sum((total > b).astype(jnp.int32) for b in BUCKETS[:-1])
    return lax.switch(which, [functools.partial(with_slots, b) for b in BUCKETS], block, weight, place)


def solution(mesh):
    in_specs = (P(None, "gvec", "band", None), P(), P(), P(), P())
    out_specs = P("gvec", "band")
    return jax.shard_map(
        on_device, mesh=mesh, in_specs=in_specs, out_specs=out_specs, check_vma=False
    )
```

```python
import functools

import jax
import jax.numpy as jnp
from jax import lax
from jax.experimental import pallas as pl
from jax.experimental.pallas import tpu as pltpu
from jax.sharding import PartitionSpec as P

BUCKETS = (288, 336, 512)
Z, X = 8, 4
WIDE = 384
VMEM_BYTES = 48 * 1024 * 1024
BOTH = ("band", "gvec")
ALONG_Z = [[z * X + x for z in range(Z)] for x in range(X)]


def band_of(z, x):
    return (z % Z) * X + x % X


def shift(value, dz, dx):
    pairs = [(band_of(z + dz, x + dx), band_of(z, x)) for z in range(Z) for x in range(X)]
    return lax.ppermute(value, "band", pairs)


def to_rows(value):
    moves = [
        (band_of(z, x) * Z + v, band_of(v, x) * Z + z)
        for z in range(Z) for x in range(X) for v in range(Z)
    ]
    return lax.ppermute(value, BOTH, moves)


def cut_of(depth):
    return depth // 32 * 16


def low_of(value):
    return value[:cut_of(value.shape[0])]


def high_of(value):
    return value[cut_of(value.shape[0]):]


def together(*values):
    return lax.optimization_barrier(values)


def from_y(value, dy):
    return lax.ppermute(value, "gvec", [((i + 2 * dy) % Z, i) for i in range(Z)])


def contract(left, right):
    return lax.dot_general(left, right, (((0,), (0,)), ((), ())), preferred_element_type=jnp.float32)


def sum_kernel(offsets, width, parts, adds, aliased, where, cols, *refs):
    refs = list(refs)
    lefts = [refs.pop(0) for _ in offsets]
    partial = refs.pop(0) if adds else None
    if aliased:
        refs.pop(0)
    out, acc, sems = refs
    total = None
    for offset, left in zip(offsets, lefts):
        term = contract(left[...], cols[offset:offset + left.shape[0], :])
        total = term if total is None else total + term
    if adds:
        total = total + partial[...]
    acc[...] = total
    copies = []
    for i in range(parts):
        start = pl.multiple_of(where[i], 128)
        copies.append(
            pltpu.make_async_copy(acc.at[pl.ds(i * width, width)], out.at[pl.ds(start, width)], sems.at[i])
        )
        copies[-1].start()
    for copy in copies:
        copy.wait()


def add_rows(out, where, cols, lefts, offsets, parts, partial=None, size=None):
    height, n = lefts[0].shape[1], cols.shape[1]
    width = height // parts
    vmem = pl.BlockSpec(memory_space=pltpu.VMEM)
    operands = [where, cols, *lefts] + ([] if partial is None else [partial])
    specs = [pl.BlockSpec(memory_space=pltpu.SMEM)] + [vmem] * (len(operands) - 1)
    alias = {}
    if out is not None:
        alias = {len(operands): 0}
        operands.append(out)
        specs.append(pl.BlockSpec(memory_space=pl.ANY))
        size = out.shape
    depth = sum(left.shape[0] for left in lefts)
    return pl.pallas_call(
        functools.partial(sum_kernel, offsets, width, parts, partial is not None, out is not None),
        out_shape=jax.ShapeDtypeStruct(size, jnp.float32),
        in_specs=specs,
        out_specs=pl.BlockSpec(memory_space=pl.ANY),
        scratch_shapes=[pltpu.VMEM((height, n), jnp.float32), pltpu.SemaphoreType.DMA((parts,))],
        input_output_aliases=alias,
        compiler_params=pltpu.CompilerParams(vmem_limit_bytes=VMEM_BYTES),
        cost_estimate=pl.CostEstimate(
            flops=2 * depth * height * n, bytes_accessed=2 * depth * (height + n) + 4 * height * n, transcendentals=0
        ),
    )(*operands)


def rows_kernel(width, parts, where, cols, rows, _, out, acc, sems):
    step = pl.program_id(0)

    def stores(at):
        copies = []
        for i in range(parts):
            start = pl.multiple_of(where[at * parts + i], 128)
            copies.append(pltpu.make_async_copy(
                acc.at[at, pl.ds(i * width, width)], out.at[pl.ds(start, width)], sems.at[at, i]
            ))
        return copies

    acc[step] = contract(rows[...].reshape(cols.shape[0], parts * width), cols[...])
    for copy in stores(step):
        copy.start()

    @pl.when(step == X // parts - 1)
    def _():
        for at in range(X // parts):
            for copy in stores(at):
                copy.wait()


def add_gathered(out, where, cols, rows):
    depth, n = rows.shape[1], cols.shape[1]
    width, parts = rows.shape[2] // X, 2
    return pl.pallas_call(
        functools.partial(rows_kernel, width, parts),
        grid=(X // parts,),
        out_shape=jax.ShapeDtypeStruct(out.shape, jnp.float32),
        in_specs=[
            pl.BlockSpec(memory_space=pltpu.SMEM),
            pl.BlockSpec(cols.shape, lambda j: (0, 0)),
            pl.BlockSpec((Z, depth, parts * width), lambda j: (0, 0, j)),
            pl.BlockSpec(memory_space=pl.ANY),
        ],
        out_specs=pl.BlockSpec(memory_space=pl.ANY),
        scratch_shapes=[
            pltpu.VMEM((X // parts, parts * width, n), jnp.float32),
            pltpu.SemaphoreType.DMA((X // parts, parts)),
        ],
        input_output_aliases={3: 0},
        compiler_params=pltpu.CompilerParams(vmem_limit_bytes=VMEM_BYTES),
        cost_estimate=pl.CostEstimate(
            flops=2 * X * Z * depth * width * n, bytes_accessed=2 * X * Z * depth * (width + n), transcendentals=0
        ),
    )(where, cols, rows, out)


def order_kernel(depth, order, half, other, out, sems):
    def copies(source, wanted):
        for i in range(Z):
            place = order[i]

            @pl.when((place >= X) == wanted)
            def _():
                start = pl.multiple_of(place % X * depth, 16)
                pltpu.make_async_copy(
                    source.at[pl.ds(start, depth)], out.at[pl.ds(i * depth, depth)], sems.at[i]
                ).start()

    copies(half, False)
    copies(other, True)
    for i in range(Z):
        pltpu.make_async_copy(half.at[pl.ds(0, depth)], out.at[pl.ds(i * depth, depth)], sems.at[i]).wait()


def reorder(order, half, other):
    depth, n = half.shape[0] // X, half.shape[1]
    return pl.pallas_call(
        functools.partial(order_kernel, depth),
        out_shape=jax.ShapeDtypeStruct((Z * depth, n), half.dtype),
        in_specs=[pl.BlockSpec(memory_space=pltpu.SMEM)] + [pl.BlockSpec(memory_space=pl.ANY)] * 2,
        out_specs=pl.BlockSpec(memory_space=pltpu.VMEM),
        scratch_shapes=[pltpu.SemaphoreType.DMA((Z,))],
        compiler_params=pltpu.CompilerParams(vmem_limit_bytes=VMEM_BYTES),
        cost_estimate=pl.CostEstimate(flops=0, bytes_accessed=4 * Z * depth * n, transcendentals=0),
    )(order, half, other)


def with_offsets(at, *lefts):
    offsets = []
    for left in lefts:
        offsets.append(at)
        at += left.shape[0]
    return lefts, offsets


def with_slots(depth, block, weight, place):
    gvec, band = lax.axis_index("gvec"), lax.axis_index("band")
    x = band % X
    n = block.shape[1]
    rows_of = jnp.arange(depth, dtype=jnp.int32)
    select = (rows_of[:, None] == place[None, :]).astype(jnp.bfloat16)
    packed = jnp.dot(select, block, preferred_element_type=jnp.float32).astype(jnp.bfloat16)
    scaled = (weight[:, None] * block.astype(jnp.float32)).astype(jnp.bfloat16)
    packed_cols = jnp.dot(select, scaled, preferred_element_type=jnp.float32).astype(jnp.bfloat16)

    a0 = to_rows(packed[:, :WIDE])
    a0, packed_b, mine = together(a0, packed[:, WIDE:], packed_cols)
    a_all = lax.all_gather(a0, "band", axis=0, axis_index_groups=ALONG_Z, tiled=True)
    b0 = to_rows(packed_b)

    b1, b3 = shift(b0, 0, 1), shift(b0, 0, -1)
    y2 = from_y(mine, 2)
    b1, b3, y2 = together(b1, b3, y2)
    b2 = jnp.concatenate([shift(low_of(b1), 0, 1), shift(high_of(b3), 0, -1)], axis=0)
    b = jnp.concatenate([b0, b1, b2, b3], axis=1)
    y1, y3 = from_y(mine, 1), from_y(mine, -1)
    b, y1, y3 = together(b, y1, y3)
    b_all = lax.all_gather(b, "band", axis=0, axis_index_groups=ALONG_Z)
    half = jnp.concatenate([mine, y1, y2, y3], axis=0)
    other = lax.ppermute(half, "gvec", [(i ^ 1, i) for i in range(Z)])

    y, core = gvec // 2, gvec % 2
    wanted = jnp.arange(Z, dtype=jnp.int32)
    cols = reorder((wanted // 2 - y + X) % X + X * (wanted % 2 != core).astype(jnp.int32), half, other)

    def starts(shifts, base):
        return jnp.stack([(x + s) % X * n + base for s in shifts]).astype(jnp.int32)

    a_all, cols = together(a_all, cols)
    near, far = shift(a_all, 0, 1), shift(a_all, 0, -1)
    out = add_rows(None, starts([0], 0), cols, *with_offsets(0, a_all), 1, size=(X * n, n))
    near, far, out = together(near, far, out)

    low, high = shift(low_of(near), 0, 1), shift(high_of(far), 0, -1)
    out = add_rows(out, starts([1], 0), cols, *with_offsets(0, near), 1)
    out = add_rows(out, starts([3], 0), cols, *with_offsets(0, far), 1)
    out = add_gathered(out, starts([0, 1, 2, 3], WIDE), cols, b_all)
    return add_rows(out, starts([2], 0), cols, *with_offsets(0, low, high), 1)


def on_device(pairs, cond_energy, val_energy, band_counts, slab):
    gvec = lax.axis_index("gvec")
    blocks, _, slots, n = pairs.shape
    energies = lax.dynamic_index_in_dim(val_energy, slab[0], 0, keepdims=False)
    energy = lax.dynamic_index_in_dim(energies, gvec, 0, keepdims=False)
    live = (jnp.arange(slots, dtype=jnp.int32)[None, :] < band_counts[:, None]).reshape(-1)
    weight = jnp.where(live, 2.0 / (energy - cond_energy), jnp.float32(0.0))
    owners = jnp.arange(band_counts.shape[0])
    before = jnp.sum(jnp.where(owners[None, :] < owners[:, None], band_counts[None, :], 0), axis=1)
    place = jnp.where(
        live, (before[:, None] + jnp.arange(slots, dtype=jnp.int32)[None, :]).reshape(-1), -1
    )
    total = jnp.sum(band_counts)

    block = lax.all_to_all(pairs.reshape(blocks, slots, n), "band", split_axis=0, concat_axis=0, tiled=True)
    block = block.reshape(blocks * slots, n)
    block, weight, place, total = together(block, weight, place, total)
    which = sum((total > b).astype(jnp.int32) for b in BUCKETS[:-1])
    return lax.switch(which, [functools.partial(with_slots, b) for b in BUCKETS], block, weight, place)


def solution(mesh):
    in_specs = (P(None, "gvec", "band", None), P(), P(), P(), P())
    out_specs = P("gvec", "band")
    return jax.shard_map(
        on_device, mesh=mesh, in_specs=in_specs, out_specs=out_specs, check_vma=False
    )
```

```python
import functools

import jax
import jax.numpy as jnp
from jax import lax
from jax.experimental import pallas as pl
from jax.experimental.pallas import tpu as pltpu
from jax.sharding import PartitionSpec as P

BUCKETS = (288, 336, 512)
Z, X = 8, 4
WIDE = 384
VMEM_BYTES = 48 * 1024 * 1024
BOTH = ("band", "gvec")
ALONG_Z = [[z * X + x for z in range(Z)] for x in range(X)]


def band_of(z, x):
    return (z % Z) * X + x % X


def shift(value, dz, dx):
    pairs = [(band_of(z + dz, x + dx), band_of(z, x)) for z in range(Z) for x in range(X)]
    return lax.ppermute(value, "band", pairs)


def to_rows(value):
    moves = [
        (band_of(z, x) * Z + v, band_of(v, x) * Z + z)
        for z in range(Z) for x in range(X) for v in range(Z)
    ]
    return lax.ppermute(value, BOTH, moves)


def cut_of(depth):
    return depth // 32 * 16


def low_of(value):
    return value[:cut_of(value.shape[0])]


def high_of(value):
    return value[cut_of(value.shape[0]):]


def together(*values):
    return lax.optimization_barrier(values)


def from_y(value, dy):
    return lax.ppermute(value, "gvec", [((i + 2 * dy) % Z, i) for i in range(Z)])


def contract(left, right):
    return lax.dot_general(left, right, (((0,), (0,)), ((), ())), preferred_element_type=jnp.float32)


def sum_kernel(offsets, width, parts, adds, aliased, where, cols, *refs):
    refs = list(refs)
    lefts = [refs.pop(0) for _ in offsets]
    partial = refs.pop(0) if adds else None
    if aliased:
        refs.pop(0)
    out, acc, sems = refs
    total = None
    for offset, left in zip(offsets, lefts):
        term = contract(left[...], cols[offset:offset + left.shape[0], :])
        total = term if total is None else total + term
    if adds:
        total = total + partial[...]
    acc[...] = total
    copies = []
    for i in range(parts):
        start = pl.multiple_of(where[i], 128)
        copies.append(
            pltpu.make_async_copy(acc.at[pl.ds(i * width, width)], out.at[pl.ds(start, width)], sems.at[i])
        )
        copies[-1].start()
    for copy in copies:
        copy.wait()


def add_rows(out, where, cols, lefts, offsets, parts, partial=None, size=None):
    height, n = lefts[0].shape[1], cols.shape[1]
    width = height // parts
    vmem = pl.BlockSpec(memory_space=pltpu.VMEM)
    operands = [where, cols, *lefts] + ([] if partial is None else [partial])
    specs = [pl.BlockSpec(memory_space=pltpu.SMEM)] + [vmem] * (len(operands) - 1)
    alias = {}
    if out is not None:
        alias = {len(operands): 0}
        operands.append(out)
        specs.append(pl.BlockSpec(memory_space=pl.ANY))
        size = out.shape
    depth = sum(left.shape[0] for left in lefts)
    return pl.pallas_call(
        functools.partial(sum_kernel, offsets, width, parts, partial is not None, out is not None),
        out_shape=jax.ShapeDtypeStruct(size, jnp.float32),
        in_specs=specs,
        out_specs=pl.BlockSpec(memory_space=pl.ANY),
        scratch_shapes=[pltpu.VMEM((height, n), jnp.float32), pltpu.SemaphoreType.DMA((parts,))],
        input_output_aliases=alias,
        compiler_params=pltpu.CompilerParams(vmem_limit_bytes=VMEM_BYTES),
        cost_estimate=pl.CostEstimate(
            flops=2 * depth * height * n, bytes_accessed=2 * depth * (height + n) + 4 * height * n, transcendentals=0
        ),
    )(*operands)


def rows_kernel(width, where, cols, rows, _, out, acc, sems):
    j, slot = pl.program_id(0), pl.program_id(0) % 2

    def store(step):
        start = pl.multiple_of(where[step], 128)
        return pltpu.make_async_copy(acc.at[step % 2], out.at[pl.ds(start, width)], sems.at[step % 2])

    @pl.when(j >= 2)
    def _():
        store(j - 2).wait()

    acc[slot] = contract(rows[...].reshape(cols.shape[0], width), cols[...])
    store(j).start()

    @pl.when(j == X - 1)
    def _():
        store(j - 1).wait()
        store(j).wait()


def add_gathered(out, where, cols, rows):
    depth, n = rows.shape[1], cols.shape[1]
    width = rows.shape[2] // X
    return pl.pallas_call(
        functools.partial(rows_kernel, width),
        grid=(X,),
        out_shape=jax.ShapeDtypeStruct(out.shape, jnp.float32),
        in_specs=[
            pl.BlockSpec(memory_space=pltpu.SMEM),
            pl.BlockSpec(cols.shape, lambda j: (0, 0)),
            pl.BlockSpec((Z, depth, width), lambda j: (0, 0, j)),
            pl.BlockSpec(memory_space=pl.ANY),
        ],
        out_specs=pl.BlockSpec(memory_space=pl.ANY),
        scratch_shapes=[pltpu.VMEM((2, width, n), jnp.float32), pltpu.SemaphoreType.DMA((2,))],
        input_output_aliases={3: 0},
        compiler_params=pltpu.CompilerParams(vmem_limit_bytes=VMEM_BYTES),
        cost_estimate=pl.CostEstimate(
            flops=2 * X * Z * depth * width * n, bytes_accessed=2 * X * Z * depth * (width + n), transcendentals=0
        ),
    )(where, cols, rows, out)


def order_kernel(depth, order, half, other, out, sems):
    def copies(source, wanted):
        for i in range(Z):
            place = order[i]

            @pl.when((place >= X) == wanted)
            def _():
                start = pl.multiple_of(place % X * depth, 16)
                pltpu.make_async_copy(
                    source.at[pl.ds(start, depth)], out.at[pl.ds(i * depth, depth)], sems.at[i]
                ).start()

    copies(half, False)
    copies(other, True)
    for i in range(Z):
        pltpu.make_async_copy(half.at[pl.ds(0, depth)], out.at[pl.ds(i * depth, depth)], sems.at[i]).wait()


def reorder(order, half, other):
    depth, n = half.shape[0] // X, half.shape[1]
    return pl.pallas_call(
        functools.partial(order_kernel, depth),
        out_shape=jax.ShapeDtypeStruct((Z * depth, n), half.dtype),
        in_specs=[pl.BlockSpec(memory_space=pltpu.SMEM)] + [pl.BlockSpec(memory_space=pl.ANY)] * 2,
        out_specs=pl.BlockSpec(memory_space=pltpu.VMEM),
        scratch_shapes=[pltpu.SemaphoreType.DMA((Z,))],
        compiler_params=pltpu.CompilerParams(vmem_limit_bytes=VMEM_BYTES),
        cost_estimate=pl.CostEstimate(flops=0, bytes_accessed=4 * Z * depth * n, transcendentals=0),
    )(order, half, other)


def with_offsets(at, *lefts):
    offsets = []
    for left in lefts:
        offsets.append(at)
        at += left.shape[0]
    return lefts, offsets


def with_slots(depth, block, weight, place):
    gvec, band = lax.axis_index("gvec"), lax.axis_index("band")
    x = band % X
    n = block.shape[1]
    rows_of = jnp.arange(depth, dtype=jnp.int32)
    select = (rows_of[:, None] == place[None, :]).astype(jnp.bfloat16)
    packed = jnp.dot(select, block, preferred_element_type=jnp.float32).astype(jnp.bfloat16)
    scaled = (weight[:, None] * block.astype(jnp.float32)).astype(jnp.bfloat16)
    packed_cols = jnp.dot(select, scaled, preferred_element_type=jnp.float32).astype(jnp.bfloat16)

    a0 = to_rows(packed[:, :WIDE])
    a0, packed_b, mine = together(a0, packed[:, WIDE:], packed_cols)
    a_all = lax.all_gather(a0, "band", axis=0, axis_index_groups=ALONG_Z, tiled=True)
    b0 = to_rows(packed_b)

    b1, b3 = shift(b0, 0, 1), shift(b0, 0, -1)
    y2 = from_y(mine, 2)
    b1, b3, y2 = together(b1, b3, y2)
    b2 = jnp.concatenate([shift(low_of(b1), 0, 1), shift(high_of(b3), 0, -1)], axis=0)
    b = jnp.concatenate([b0, b1, b2, b3], axis=1)
    y1, y3 = from_y(mine, 1), from_y(mine, -1)
    b, y1, y3 = together(b, y1, y3)
    b_all = lax.all_gather(b, "band", axis=0, axis_index_groups=ALONG_Z)
    half = jnp.concatenate([mine, y1, y2, y3], axis=0)
    other = lax.ppermute(half, "gvec", [(i ^ 1, i) for i in range(Z)])

    y, core = gvec // 2, gvec % 2
    wanted = jnp.arange(Z, dtype=jnp.int32)
    cols = reorder((wanted // 2 - y + X) % X + X * (wanted % 2 != core).astype(jnp.int32), half, other)

    def starts(shifts, base):
        return jnp.stack([(x + s) % X * n + base for s in shifts]).astype(jnp.int32)

    a_all, cols = together(a_all, cols)
    near, far = shift(a_all, 0, 1), shift(a_all, 0, -1)
    out = add_rows(None, starts([0], 0), cols, *with_offsets(0, a_all), 1, size=(X * n, n))
    near, far, out = together(near, far, out)

    low, high = shift(low_of(near), 0, 1), shift(high_of(far), 0, -1)
    out = add_rows(out, starts([1], 0), cols, *with_offsets(0, near), 1)
    out = add_rows(out, starts([3], 0), cols, *with_offsets(0, far), 1)
    out = add_gathered(out, starts([0, 1, 2, 3], WIDE), cols, b_all)
    return add_rows(out, starts([2], 0), cols, *with_offsets(0, low, high), 1)


def on_device(pairs, cond_energy, val_energy, band_counts, slab):
    gvec = lax.axis_index("gvec")
    blocks, _, slots, n = pairs.shape
    energies = lax.dynamic_index_in_dim(val_energy, slab[0], 0, keepdims=False)
    energy = lax.dynamic_index_in_dim(energies, gvec, 0, keepdims=False)
    live = (jnp.arange(slots, dtype=jnp.int32)[None, :] < band_counts[:, None]).reshape(-1)
    weight = jnp.where(live, 2.0 / (energy - cond_energy), jnp.float32(0.0))
    owners = jnp.arange(band_counts.shape[0])
    before = jnp.sum(jnp.where(owners[None, :] < owners[:, None], band_counts[None, :], 0), axis=1)
    place = jnp.where(
        live, (before[:, None] + jnp.arange(slots, dtype=jnp.int32)[None, :]).reshape(-1), -1
    )
    total = jnp.sum(band_counts)

    block = lax.all_to_all(pairs.reshape(blocks, slots, n), "band", split_axis=0, concat_axis=0, tiled=True)
    block = block.reshape(blocks * slots, n)
    block, weight, place, total = together(block, weight, place, total)
    which = sum((total > b).astype(jnp.int32) for b in BUCKETS[:-1])
    return lax.switch(which, [functools.partial(with_slots, b) for b in BUCKETS], block, weight, place)


def solution(mesh):
    in_specs = (P(None, "gvec", "band", None), P(), P(), P(), P())
    out_specs = P("gvec", "band")
    return jax.shard_map(
        on_device, mesh=mesh, in_specs=in_specs, out_specs=out_specs, check_vma=False
    )
```
